128 devices in a mesh: gx: 4 (over y), gy: 16 (over x_hi, z, core), gz: 2 (over x_lo).
Axes of the slice: x: 4 (x_hi: 2, x_lo: 2; x = x_hi * 2 + x_lo), y: 4, z: 4, core: 2. Of those that a mesh axis runs over, the one named last changes fastest.
Arguments:
- inputs: bfloat16 [64, 16, 128, 256], P(None, 'gx', 'gy', 'gz'), may hold values from -6 to 6
- weight: bfloat16 [4, 4, 4, 64, 32], replicated, may hold values from -0.25 to 0.25
- cotangent: bfloat16 [2, 2, 2, 32, 16, 128, 256], P(None, None, None, None, 'gx', 'gy', 'gz'), may hold values from -3 to 3
Outputs:
- upsampled: bfloat16 [2, 2, 2, 32, 16, 128, 256], P(None, None, None, None, 'gx', 'gy', 'gz')
- input_grad: bfloat16 [64, 16, 128, 256], P(None, 'gx', 'gy', 'gz')
- weight_grad: float32 [4, 4, 4, 64, 32], replicated
The draws below stay inside these ranges and needn't reach their ends.
All inputs are finite; a program needn't handle non-finite values.
Results may differ from the reference program's by a relative error of at most 0.0018.
Values may be sent and summed in bfloat16 or wider, within the bound.
No kernel may reach another device: no remote copies, remote signals or barrier semaphores. Data moves between devices by JAX's collectives and lax.ppermute only.
A program may use at most 192 MiB of HBM per device.

```python
import math
import jax
import jax.numpy as jnp
from jax import lax

CIN = 64
COUT = 32
K = 4
NX = 16
NY = 128
NZ = 256


def level_of(rng, shape, pieces, smallest, high):
    factor_of, own = 1.0, jax.random.fold_in(rng, 6)
    for dim, blocks in pieces:
        steps = jnp.exp(jax.random.uniform(jax.random.fold_in(own, dim), (blocks,), jnp.float32, smallest / len(pieces), high / len(pieces)))
        factor_of = factor_of * jnp.repeat(steps, shape[dim] // blocks).reshape([-1 if axis == dim else 1 for axis in range(len(shape))])
    return factor_of


def scatter_about(rng, extent, scale, bound, pieces=(), kind=jnp.bfloat16):
    values = scale * jax.random.normal(rng, extent, jnp.float32)
    if pieces:
        values = values * level_of(rng, extent, pieces, -0.22, 0.18)
    return jnp.clip(values, -bound, bound).astype(kind)


def setup_inputs(seed: int = 0) -> dict:
    key_list = jax.random.split(jax.random.key(seed), 4)
    return {
        "inputs": scatter_about(key_list[0], (CIN, NX, NY, NZ), 1.0, 6.0, ((1, 4), (2, 16), (3, 2))),
        "weight": scatter_about(key_list[1], (K, K, K, CIN, COUT), (8 * CIN) ** -0.5, 0.25),
        "cotangent": scatter_about(key_list[2], (2, 2, 2, COUT, NX, NY, NZ), 0.5, 3.0, ((4, 4), (5, 16), (6, 2))),
    }


def transposed(inputs_wide, weight_wide):
    padded = jnp.pad(inputs_wide, ((0, 0), (1, 1), (1, 1), (0, 0)), mode='wrap')
    kernel = jnp.transpose(jnp.flip(weight_wide, (0, 1, 2)), (4, 3, 0, 1, 2))
    result = lax.conv_general_dilated(padded[None], kernel, (1, 1, 1), ((0, 0), (0, 0), (2, 2)), lhs_dilation=(2, 2, 2), dimension_numbers=('NCDHW', 'OIDHW', 'NCDHW'), precision=lax.Precision.HIGHEST)
    return result[0]

def to_subpixel(full):
    channels = full.shape[0]
    split = full.reshape((channels, NX, 2, NY, 2, NZ, 2))
    return split.transpose(2, 4, 6, 0, 1, 3, 5)

def from_subpixel(packed):
    channels = packed.shape[3]
    moved = packed.transpose(3, 4, 0, 5, 1, 6, 2)
    return moved.reshape((channels, 2 * NX, 2 * NY, 2 * NZ))

def reference(inputs, weight, cotangent):
    inputs_wide = inputs.astype(jnp.float32)
    weight_wide = weight.astype(jnp.float32)
    result, pullback = jax.vjp(transposed, inputs_wide, weight_wide)
    input_grad, weight_grad = pullback(from_subpixel(cotangent.astype(jnp.float32)))
    factor = 1.0 / math.sqrt(NX * NY * NZ)
    return (to_subpixel(result).astype(jnp.bfloat16), input_grad.astype(jnp.bfloat16), weight_grad * factor)
```

```python
import functools
import math

import jax
import jax.numpy as jnp
from jax import lax
from jax.experimental import pallas as pl
from jax.experimental.pallas import tpu as pltpu
from jax.sharding import PartitionSpec as P

AXES = ("gx", "gy", "gz")
F32, BF16 = jnp.float32, jnp.bfloat16
NT = (((1,), (1,)), ((), ()))
NN = (((1,), (0,)), ((), ()))
PARAMS = pltpu.CompilerParams(vmem_limit_bytes=56 * 1024 * 1024)
WHOLE = pl.BlockSpec(memory_space=pltpu.VMEM)


def shaped(shape, dtype=BF16):
    return jax.ShapeDtypeStruct(shape, dtype)


def call(kernel, out_shape, scratch=(), flops=0):
    def run(*operands):
        moved = sum(o.size * o.dtype.itemsize for o in (*operands, *jax.tree.leaves(out_shape)))
        return pl.pallas_call(
            kernel,
            out_shape=out_shape,
            in_specs=[WHOLE] * len(operands),
            out_specs=jax.tree.map(lambda _: WHOLE, out_shape),
            scratch_shapes=list(scratch),
            compiler_params=PARAMS,
            cost_estimate=pl.CostEstimate(flops=flops, bytes_accessed=moved, transcendentals=0),
        )(*operands)

    return run


def rolled(tile, column, before):
    lane = lax.broadcasted_iota(jnp.int32, tile.shape, 1)
    inside = lax.axis_index("gz") == (1 if before else 0)
    edge = jnp.where(inside, column.astype(F32), jnp.zeros(column.shape, F32))
    moved = pltpu.roll(tile, 1 if before else 127, 1).astype(F32)
    return jnp.where(lane == (0 if before else 127), edge, moved).astype(tile.dtype)


def plane_of(xe, own, left, right, z_own):
    if xe == 0:
        return left, left[:, 1024:1152]
    if xe == 5:
        return right, right[:, 1024:1152]
    return own.at[xe - 1], z_own[xe - 1]


def xor_pairs(fx, fy, fz):
    pairs = []
    for gx in range(4):
        for gy in range(16):
            for gz in range(2):
                pairs.append(((gx * 16 + gy) * 2 + gz, ((gx ^ fx) * 16 + (gy ^ fy)) * 2 + (gz ^ fz)))
    return pairs


def ring(count, step):
    return [(i, (i + step) % count) for i in range(count)]


OUTER = [(i, (i - 1) % 16 if i % 2 == 0 else (i + 1) % 16) for i in range(16)]
INNER = [(i, i ^ 1) for i in range(16)]


def first_core():
    return lax.rem(lax.axis_index("gy"), 2) == 0


def low_and_high(inner, outer, n):
    a, b, first = inner[n], outer[n], first_core()
    return jnp.where(first, b, a), jnp.where(first, a, b)


def side_picker():
    cell = lax.broadcasted_iota(jnp.int32, (1024, 128), 0)
    lane = lax.broadcasted_iota(jnp.int32, (1024, 128), 1)
    side = jnp.where(lax.axis_index("gz") == 0, 127, 0)
    return (cell == lane * 128 + side).astype(F32).astype(BF16)


def prepare_in_kernel(raw, own, z_face):
    pick = side_picker()
    for x in range(4):
        plane = raw[:, x].reshape(64, 1024)
        own[x] = plane
        z_face[x] = jnp.dot(plane, pick, preferred_element_type=F32).astype(BF16)


def prepare_cot_kernel(raw, cot, z_face):
    pick = side_picker()
    for n in range(8):
        cot[0, n * 32 : n * 32 + 32, :] = raw[n, :, 0].reshape(32, 1024)
    z_face[0] = jnp.dot(cot[0], pick, preferred_element_type=F32).astype(BF16)


def edge_in_kernel(own, left, right, z_own, inner_out, outer_out):
    lane = lax.broadcasted_iota(jnp.int32, (64, 128), 1)
    first = first_core()
    z_inner = jnp.zeros((64, 128), F32)
    z_outer = jnp.zeros((64, 128), F32)
    for xe in range(6):
        plane, z_tile = plane_of(xe, own, left, right, z_own)
        low, high = plane[:, 0:128], plane[:, 896:1024]
        inner_out[xe] = jnp.where(first, high, low)
        outer_out[xe] = jnp.where(first, low, high)
        z_wide = z_tile.astype(F32)
        low, high = z_wide[:, 0:1], z_wide[:, 7:8]
        z_inner = jnp.where(lane == xe, jnp.where(first, high, low), z_inner)
        z_outer = jnp.where(lane == xe, jnp.where(first, low, high), z_outer)
    inner_out[6] = z_inner.astype(BF16)
    outer_out[6] = z_outer.astype(BF16)


def cot_rows(n, py, own, left, right, z_own):
    xe, px = (n + 1) // 2, (n + 1) % 2
    if xe == 0 or xe == 5:
        part = left if xe == 0 else right
        rows = slice(py * 64, py * 64 + 64)
        return lambda y: part[rows, y * 128 : y * 128 + 128], part[rows, 1024:1152]
    rows = slice(px * 128 + py * 64, px * 128 + py * 64 + 64)
    return lambda y: own[xe - 1, rows, y * 128 : y * 128 + 128], z_own[xe - 1, rows, :]


def edge_cot_kernel(own, left, right, z_own, inner_out, outer_out):
    lane = lax.broadcasted_iota(jnp.int32, (64, 128), 1)
    first = first_core()
    z_inner = jnp.zeros((64, 128), F32)
    z_outer = jnp.zeros((64, 128), F32)
    for n in range(10):
        cells, z_tile = cot_rows(n, 0, own, left, right, z_own)
        low, z_low = cells(0), z_tile.astype(F32)[:, 0:1]
        cells, z_tile = cot_rows(n, 1, own, left, right, z_own)
        high, z_high = cells(7), z_tile.astype(F32)[:, 7:8]
        inner_out[n] = jnp.where(first, high, low)
        outer_out[n] = jnp.where(first, low, high)
        z_inner = jnp.where(lane == n, jnp.where(first, z_high, z_low), z_inner)
        z_outer = jnp.where(lane == n, jnp.where(first, z_low, z_high), z_outer)
    inner_out[10] = z_inner.astype(BF16)
    outer_out[10] = z_outer.astype(BF16)


def fill_windows(planes, own, left, right, z_own, windows, edges=None):
    for spot, xe in enumerate(planes):
        plane, z_tile = plane_of(xe, own, left, right, z_own)
        base = spot * 576
        for y in range(8):
            tile = plane[:, y * 128 : y * 128 + 128]
            column = z_tile[:, y : y + 1]
            three = (rolled(tile, column, True), tile, rolled(tile, column, False))
            for sz in range(3):
                for sy in range(3):
                    at = y - (sy - 1)
                    if 0 <= at < 8:
                        row = base + sy * 192 + sz * 64
                        windows[row : row + 64, at * 128 : at * 128 + 128] = three[sz]
        if edges is None:
            nothing = jnp.zeros((192, 128), BF16)
            windows[base : base + 192, 0:128] = nothing
            windows[base + 384 : base + 576, 896:1024] = nothing
        else:
            for edge, row, cells in ((0, base, slice(0, 128)), (1, base + 384, slice(896, 1024))):
                tile = low_and_high(*edges, xe)[edge]
                column = low_and_high(*edges, 6)[edge][:, xe : xe + 1]
                windows[row : row + 64, cells] = rolled(tile, column, True)
                windows[row + 64 : row + 128, cells] = tile
                windows[row + 128 : row + 192, cells] = rolled(tile, column, False)


def wgrad_main_kernel(own, left, right, z_own, cot, pay_out, windows, total):
    fill_windows(range(6), own, left, right, z_own, windows)
    for x in range(4):
        part = lax.dot_general(windows[x * 576 : x * 576 + 1728, :], cot[x], NT, preferred_element_type=F32)
        if x == 0:
            total[...] = part
        else:
            total[...] += part
    lane = lax.broadcasted_iota(jnp.int32, (64, 128), 1) // 32
    for px in range(2):
        for hx in range(2):
            for hy in range(2):
                for hz in range(2):
                    block = jnp.zeros((64, 128), F32)
                    for py in range(2):
                        for pz in range(2):
                            row = ((px - hx + 1) * 9 + (py - hy + 1) * 3 + (pz - hz + 1)) * 64
                            piece = total[row : row + 64, px * 128 : px * 128 + 128]
                            block = piece if py + pz == 0 else jnp.where(lane == 2 * py + pz, piece, block)
                    at = (px * 8 + hx * 4 + hy * 2 + hz) * 64
                    pay_out[at : at + 64, :] = block


def wgrad_edge_kernel(inner, outer, cot, pay, keep, give, edges):
    first = first_core()
    for xe in range(6):
        for edge in range(2):
            tile = low_and_high(inner, outer, xe)[edge]
            column = low_and_high(inner, outer, 6)[edge][:, xe : xe + 1]
            base = xe * 192
            edges[edge, base : base + 64, :] = rolled(tile, column, True)
            edges[edge, base + 64 : base + 128, :] = tile
            edges[edge, base + 128 : base + 192, :] = rolled(tile, column, False)
    sums = []
    for edge, cells in ((0, slice(0, 128)), (1, slice(896, 1024))):
        summed = None
        for x in range(4):
            part = lax.dot_general(
                edges[edge, x * 192 : x * 192 + 576, :], cot[x, :, cells], NT, preferred_element_type=F32
            )
            summed = part if summed is None else summed + part
        sums.append(summed)
    lane = lax.broadcasted_iota(jnp.int32, (64, 128), 1) // 32
    for hx in range(2):
        for hy in range(2):
            for hz in range(2):
                at = (hx * 4 + hy * 2 + hz) * 64
                blocks = []
                for px in range(2):
                    block = pay[px * 512 + at : px * 512 + at + 64, :]
                    for py in range(2):
                        if py - hy == 0:
                            continue
                        for pz in range(2):
                            row = ((px - hx + 1) * 3 + (pz - hz + 1)) * 64
                            piece = sums[0 if py - hy < 0 else 1][row : row + 64, px * 128 : px * 128 + 128]
                            block = jnp.where(lane == 2 * py + pz, block + piece, block)
                    blocks.append(block)
                keep[at : at + 64, :] = jnp.where(first, blocks[0], blocks[1])
                give[at : at + 64, :] = jnp.where(first, blocks[1], blocks[0])


def z_bit():
    chip = lax.rem(lax.axis_index("gy") // 2, 4)
    return lax.rem(chip, 2) ^ (chip // 2)


def finish_kernel(mine, beside, other, other_beside, out, *, factor):
    first, low = first_core(), z_bit() == 0
    for hx in range(2):
        for hy in range(2):
            for hz in range(2):
                at = (hy * 2 + hz) * 64
                own = jnp.where(low == (hx == 0), mine[at : at + 64, :], beside[at : at + 64, :])
                far = jnp.where(low == (hx == 0), other[at : at + 64, :], other_beside[at : at + 64, :])
                for px in range(2):
                    block = (jnp.where(first == (px == 0), own, far) * factor).T
                    for py in range(2):
                        for pz in range(2):
                            spot = (2 * py + pz) * 32
                            out[2 * hx + 1 - px, 2 * hy + 1 - py, 2 * hz + 1 - pz] = block[spot : spot + 32, :]


def up_kernel(own, left, right, z_own, inner, outer, weight, out, windows, matrix, *, start):
    taps = ((3, 1, None), (None, 2, 0))
    fill_windows(range(start, start + 4), own, left, right, z_own, windows, (inner, outer))
    for px in range(2):
        for py in range(2):
            for pz in range(2):
                pieces = []
                for kx in taps[px]:
                    for ky in taps[py]:
                        for kz in taps[pz]:
                            if kx is None or ky is None or kz is None:
                                pieces.append(jnp.zeros((32, 64), BF16))
                            else:
                                pieces.append(weight[kx, ky, kz])
                row = (px * 4 + py * 2 + pz) * 32
                matrix[row : row + 32, :] = jnp.concatenate(pieces, axis=1)
    for x in range(2):
        result = lax.dot_general(matrix[...], windows[x * 576 : x * 576 + 1728, :], NN, preferred_element_type=F32)
        for n in range(8):
            out[n, :, x] = result[n * 32 : n * 32 + 32].astype(BF16).reshape(32, 8, 128)


def igrad_kernel(own, left, right, z_own, inner, outer, weight, out, windows, matrix, *, start):
    for spot in range(6):
        n = 2 * start + spot
        for ky in range(4):
            py, sy = ((1, -1), (0, 0), (1, 0), (0, 1))[ky]
            cells_at, z_tile = cot_rows(n, py, own, left, right, z_own)
            base = spot * 512 + ky * 128
            for y in range(8):
                source = y + sy
                if 0 <= source < 8:
                    tile, column = cells_at(source), z_tile[:, source : source + 1]
                else:
                    edge = 0 if sy < 0 else 1
                    tile = low_and_high(inner, outer, n)[edge]
                    column = low_and_high(inner, outer, 10)[edge][:, n : n + 1]
                cells = slice(y * 128, y * 128 + 128)
                windows[base : base + 64, cells] = tile
                windows[base + 64 : base + 96, cells] = rolled(tile[0:32], column[0:32], False)
                windows[base + 96 : base + 128, cells] = rolled(tile[32:64], column[32:64], True)
    for kx in range(4):
        for ky in range(4):
            row = (kx * 4 + ky) * 128
            for place, kz in enumerate((1, 2, 3, 0)):
                matrix[row + place * 32 : row + place * 32 + 32, :] = weight[kx, ky, kz]
    turned = matrix[...].T
    for x in range(2):
        result = lax.dot_general(turned, windows[x * 1024 : x * 1024 + 2048, :], NN, preferred_element_type=F32)
        out[:, x] = result.astype(BF16).reshape(64, 8, 128)


def send(block, *flip):
    return lax.ppermute(block, AXES, xor_pairs(*flip))


def beside(block, flip, work):
    run, operands = work
    block, operands = lax.optimization_barrier((block, operands))
    got = send(block, *flip)
    return lax.optimization_barrier((block, got, run(*operands)))


def body(inputs, weight, cotangent):
    x_up, x_down = ring(4, 1), ring(4, -1)
    swap = [(0, 1), (1, 0)]
    weight_t = weight.transpose(0, 1, 2, 4, 3)

    own, z_face = call(prepare_in_kernel, (shaped((4, 64, 1024)), shaped((4, 64, 128))))(inputs)
    z_own = lax.ppermute(z_face, "gz", swap)
    cot, z_face = pl.pallas_call(
        prepare_cot_kernel,
        grid=(4,),
        out_shape=(shaped((4, 256, 1024)), shaped((4, 256, 128))),
        in_specs=[pl.BlockSpec((8, 32, 1, 8, 128), lambda x: (0, 0, x, 0, 0))],
        out_specs=(pl.BlockSpec((1, 256, 1024), lambda x: (x, 0, 0)), pl.BlockSpec((1, 256, 128), lambda x: (x, 0, 0))),
        compiler_params=PARAMS,
    )(cotangent.reshape(8, 32, 4, 8, 128))
    z_cot = lax.ppermute(z_face, "gz", swap)
    left = lax.ppermute(jnp.concatenate([own[3], z_own[3]], axis=1), "gx", x_up)
    right = lax.ppermute(jnp.concatenate([own[0], z_own[0]], axis=1), "gx", x_down)
    cot_left = lax.ppermute(jnp.concatenate([cot[3, 128:], z_cot[3, 128:]], axis=1), "gx", x_up)
    cot_right = lax.ppermute(jnp.concatenate([cot[0, :128], z_cot[0, :128]], axis=1), "gx", x_down)

    inner, outer = call(edge_in_kernel, (shaped((7, 64, 128)),) * 2)(own, left, right, z_own)
    outer = lax.ppermute(outer, "gy", OUTER)
    inner = lax.ppermute(inner, "gy", INNER)
    pay = call(
        wgrad_main_kernel,
        shaped((1024, 128), F32),
        [pltpu.VMEM((3456, 1024), BF16), pltpu.VMEM((1728, 256), F32)],
        flops=2 * 1728 * 256 * 4096,
    )(own, left, right, z_own, cot)
    keep, give = call(
        wgrad_edge_kernel, (shaped((512, 128), F32),) * 2, [pltpu.VMEM((2, 1152, 128), BF16)], flops=2 * 1152 * 256 * 512
    )(inner, outer, cot, pay)

    def up_part(start):
        return call(
            functools.partial(up_kernel, start=start),
            shaped((8, 32, 2, 8, 128)),
            [pltpu.VMEM((2304, 1024), BF16), pltpu.VMEM((256, 1728), BF16)],
            flops=2 * 1728 * 256 * 2048,
        ), (own, left, right, z_own, inner, outer, weight_t)

    def igrad_part(start):
        return call(
            functools.partial(igrad_kernel, start=start),
            shaped((64, 2, 8, 128)),
            [pltpu.VMEM((3072, 1024), BF16), pltpu.VMEM((2048, 64), BF16)],
            flops=2 * 2048 * 256 * 2048,
        ), (cot, cot_left, cot_right, z_cot, cot_inner, cot_outer, weight_t)

    block = keep + send(give, 0, 1, 0)
    half = block.shape[0] // 2
    low = z_bit() == 0
    keep, give = jnp.where(low, block[:half], block[half:]), jnp.where(low, block[half:], block[:half])
    edge_cot = call(edge_cot_kernel, (shaped((11, 64, 128)),) * 2), (cot, cot_left, cot_right, z_cot)
    _, got, (cot_inner, cot_outer) = beside(give, (0, 2, 0), edge_cot)
    block = keep + got
    cot_outer = lax.ppermute(cot_outer, "gy", OUTER)
    cot_inner = lax.ppermute(cot_inner, "gy", INNER)
    block, got, up_0 = beside(block, (0, 6, 0), up_part(0))
    block = block + got
    block, got, up_1 = beside(block, (1, 0, 0), up_part(2))
    block = block + got
    block, got, grad_0 = beside(block, (3, 0, 0), igrad_part(0))
    block = block + got
    block, got, grad_1 = beside(block, (0, 0, 1), igrad_part(2))
    block = block + got

    def join(a, b, c, d):
        return jnp.concatenate([a, b], axis=2), jnp.concatenate([c, d], axis=1)

    block, got, (up, grad) = beside(block, (0, 8, 1), (join, (up_0, up_1, grad_0, grad_1)))
    block = block + got
    near = send(block, 0, 2, 0)
    factor = 1.0 / math.sqrt(4 * 16 * 2 * inputs.shape[1] * inputs.shape[2] * inputs.shape[3])
    weight_grad = call(functools.partial(finish_kernel, factor=factor), shaped((4, 4, 4, 32, 64), F32))(
        block, near, send(block, 0, 1, 0), send(near, 0, 1, 0)
    )
    return up.reshape(2, 2, 2, 32, 4, 8, 128), grad, weight_grad.transpose(0, 1, 2, 4, 3)


def solution(mesh):
    placed = (P(None, "gx", "gy", "gz"), P(), P(None, None, None, None, "gx", "gy", "gz"))
    return jax.shard_map(
        body,
        mesh=mesh,
        in_specs=placed,
        out_specs=(P(None, None, None, None, "gx", "gy", "gz"), P(None, "gx", "gy", "gz"), P()),
        check_vma=False,
    )
```

```python
import functools
import math

import jax
import jax.numpy as jnp
from jax import lax
from jax.experimental import pallas as pl
from jax.experimental.pallas import tpu as pltpu
from jax.sharding import PartitionSpec as P

AXES = ("gx", "gy", "gz")
F32, BF16 = jnp.float32, jnp.bfloat16
NT = (((1,), (1,)), ((), ()))
NN = (((1,), (0,)), ((), ()))
PARAMS = pltpu.CompilerParams(vmem_limit_bytes=24 * 1024 * 1024)
WHOLE = pl.BlockSpec(memory_space=pltpu.VMEM)
FAR = pl.BlockSpec(memory_space=pltpu.HBM)


def shaped(shape, dtype=BF16):
    return pltpu.VMEM(shape, dtype)


def call(kernel, out_shape, scratch=(), flops=0, far=(), aliases=None):
    def run(*operands):
        moved = sum(math.prod(o.shape) * o.dtype.itemsize for o in (*operands, *jax.tree.leaves(out_shape)))
        return pl.pallas_call(
            kernel,
            out_shape=out_shape,
            in_specs=[FAR if n in far else WHOLE for n in range(len(operands))],
            out_specs=jax.tree.map(lambda o: FAR if isinstance(o, jax.ShapeDtypeStruct) else WHOLE, out_shape),
            scratch_shapes=list(scratch),
            compiler_params=PARAMS,
            input_output_aliases=aliases or {},
            cost_estimate=pl.CostEstimate(flops=flops, bytes_accessed=moved, transcendentals=0),
        )(*[pltpu.with_memory_space_constraint(o, pltpu.HBM if n in far else pltpu.VMEM) for n, o in enumerate(operands)])

    return run


def rolled(tile, column, before):
    lane = lax.broadcasted_iota(jnp.int32, tile.shape, 1)
    inside = lax.axis_index("gz") == (1 if before else 0)
    edge = jnp.where(inside, column.astype(F32), jnp.zeros(column.shape, F32))
    moved = pltpu.roll(tile, 1 if before else 127, 1).astype(F32)
    return jnp.where(lane == (0 if before else 127), edge, moved).astype(tile.dtype)


def plane_of(xe, own, left, right, low, high, z_all):
    if xe == 0 or xe == 5:
        plane, lane = (left, 1310) if xe == 0 else (right, 1280)
        return lambda ye: (plane[:, ye * 128 : ye * 128 + 128], plane[:, lane + ye : lane + ye + 1])

    def at(ye):
        column = z_all[:, xe * 10 - 10 + ye : xe * 10 - 9 + ye]
        if ye == 0 or ye == 9:
            return (low if ye == 0 else high)[xe - 1], column
        return own[xe - 1, :, ye * 128 - 128 : ye * 128], column

    return at


def xor_pairs(fx, fy, fz):
    pairs = []
    for gx in range(4):
        for gy in range(16):
            for gz in range(2):
                pairs.append(((gx * 16 + gy) * 2 + gz, ((gx ^ fx) * 16 + (gy ^ fy)) * 2 + (gz ^ fz)))
    return pairs


def ring(count, step):
    return [(i, (i + step) % count) for i in range(count)]


OUTER = [(i, (i - 1) % 16 if i % 2 == 0 else (i + 1) % 16) for i in range(16)]
INNER = [(i, i ^ 1) for i in range(16)]


def first_core():
    return lax.rem(lax.axis_index("gy"), 2) == 0


def low_and_high(inner, outer, n):
    a, b, first = inner[n], outer[n], first_core()
    return jnp.where(first, b, a), jnp.where(first, a, b)


def side_picker(x):
    cell = lax.broadcasted_iota(jnp.int32, (1024, 128), 0)
    lane = lax.broadcasted_iota(jnp.int32, (1024, 128), 1)
    side = jnp.where(lax.axis_index("gz") == 0, 127, 0)
    return (cell == (lane - 10 * x - 1) * 128 + side).astype(F32).astype(BF16)


def prepare_in_kernel(raw, own, z_face, inner, outer, arrived, sems):
    copies = [pltpu.make_async_copy(raw.at[16 * n : 16 * n + 16], arrived.at[16 * n : 16 * n + 16], sems.at[n]) for n in range(4)]
    for copy in copies:
        copy.start()
    for copy in copies:
        copy.wait()
    faces = jnp.zeros((64, 128), F32)
    for x in range(4):
        plane = arrived[:, x].reshape(64, 1024)
        own[x] = plane
        low, high = plane[:, 0:128], plane[:, 896:1024]
        inner[x] = jnp.where(first_core(), high, low)
        outer[x] = jnp.where(first_core(), low, high)
        faces += jnp.dot(plane, side_picker(x), preferred_element_type=F32)
    z_face[...] = faces.astype(BF16)


def prepare_cot_kernel(raw, cot, z_face, inner, outer, arrived, sems):
    copies = [pltpu.make_async_copy(raw.at[n], arrived.at[n], sems.at[n]) for n in range(8)]
    for copy in copies:
        copy.start()
    for n in range(8):
        copies[n].wait()
        for x in range(4):
            cot[x, n * 32 : n * 32 + 32, :] = arrived[n, :, x].reshape(32, 1024)
    faces = jnp.zeros((256, 128), F32)
    for x in range(4):
        faces += jnp.dot(cot[x], side_picker(x), preferred_element_type=F32)
        for px in range(2):
            row = px * 128
            low, high = cot[x, row : row + 64, 0:128], cot[x, row + 64 : row + 128, 896:1024]
            inner[x, px * 64 : px * 64 + 64, :] = jnp.where(first_core(), high, low)
            outer[x, px * 64 : px * 64 + 64, :] = jnp.where(first_core(), low, high)
    odd = lax.axis_index("gz") == 0
    for n in range(4):
        even_rows, odd_rows = faces[n * 64 : n * 64 + 32], faces[n * 64 + 32 : n * 64 + 64]
        z_face[n * 32 : n * 32 + 32, :] = jnp.where(odd, odd_rows, even_rows).astype(BF16)


def side_in_kernel(own, z_own, inner, outer, up, down, low, high, z_all):
    lane = lax.broadcasted_iota(jnp.int32, (64, 128), 1)
    z_low, z_high = (tile.astype(F32) for tile in low_and_high(inner, outer, slice(256, 320)))
    every = z_own[...].astype(F32)
    for x in range(4):
        low[x], high[x] = low_and_high(inner, outer, slice(x * 64, x * 64 + 64))
        every = jnp.where(lane == x * 10, z_low[:, x * 10 + 8 : x * 10 + 9], every)
        every = jnp.where(lane == x * 10 + 9, z_high[:, x * 10 + 1 : x * 10 + 2], every)
    z_all[...] = every.astype(BF16)
    for x, out in ((0, down), (3, up)):
        out[:, 0:128] = low[x]
        out[:, 128:1152] = own[x]
        out[:, 1152:1280] = high[x]
        out[:, 1280:1408] = z_all[...]


def side_cot_kernel(cot, z_face, inner, outer, up, down, low, high, z_out):
    lane = lax.broadcasted_iota(jnp.int32, (32, 128), 1)
    odd = lax.axis_index("gz") == 0
    for x in range(4):
        low[x], high[x] = low_and_high(inner, outer, slice(320 + x * 128, 448 + x * 128))
    for px in range(2):
        for py, side, spot in ((0, high, 9), (1, low, 0)):
            rows = slice((px * 2 + py) * 32, (px * 2 + py) * 32 + 32)
            face = z_face[rows, :].astype(F32)
            for x in range(4):
                even_rows, odd_rows = side[x, px * 64 : px * 64 + 32, :], side[x, px * 64 + 32 : px * 64 + 64, :]
                column = jnp.where(odd, odd_rows[:, 127:128].astype(F32), even_rows[:, 0:1].astype(F32))
                face = jnp.where(lane == x * 10 + spot, column, face)
            z_out[rows, :] = face.astype(BF16)
    nothing = jnp.zeros((64, 128), BF16)
    for x, px, out in ((0, 0, down), (3, 1, up)):
        out[0:64, 0:128] = nothing
        out[64:128, 0:128] = low[x, px * 64 : px * 64 + 64, :]
        out[:, 128:1152] = cot[x, px * 128 : px * 128 + 128, :]
        out[0:64, 1152:1280] = high[x, px * 64 : px * 64 + 64, :]
        out[64:128, 1152:1280] = nothing


def cot_plane_of(n, py, own, left, right, low, high, z_all):
    xe, px = (n + 1) // 2, (n + 1) % 2
    if xe == 0 or xe == 5:
        part, lane = (left, 1310) if xe == 0 else (right, 1280)
        rows, halo = slice(py * 64, py * 64 + 64), slice(py * 32, py * 32 + 32)
        return lambda ye: (part[rows, ye * 128 : ye * 128 + 128], part[halo, lane + ye : lane + ye + 1])

    def at(ye):
        row = (px * 2 + py) * 32
        column = z_all[row : row + 32, xe * 10 - 10 + ye : xe * 10 - 9 + ye]
        if ye == 0 or ye == 9:
            return (low if ye == 0 else high)[xe - 1, px * 64 : px * 64 + 64, :], column
        row = px * 128 + py * 64
        return own[xe - 1, row : row + 64, ye * 128 - 128 : ye * 128], column

    return at


def fill_windows(planes, block, windows):
    for spot, xe in enumerate(planes):
        plane = plane_of(xe, *block)
        for ye in range(10):
            tile, column = plane(ye)
            three = (rolled(tile, column, True), tile, rolled(tile, column, False))
            for sy in range(3):
                at = ye - sy
                if 0 <= at < 8:
                    for sz in range(3):
                        row = spot * 576 + sy * 192 + sz * 64
                        windows[row : row + 64, at * 128 : at * 128 + 128] = three[sz]


def wgrad_main_kernel(own, low, high, z_all, cot, pay_out, windows, total):
    fill_windows(range(1, 5), (own, None, None, low, high, z_all), windows)
    for x in (1, 0, 2, 3):
        first, last = max(x - 1, 0), min(x + 1, 3)
        part = lax.dot_general(windows[first * 576 : last * 576 + 576, :], cot[x], NT, preferred_element_type=F32)
        if x == 1:
            total[...] = part
        else:
            row = (first - x + 1) * 576
            total[row : row + part.shape[0], :] += part
    lane = lax.broadcasted_iota(jnp.int32, (64, 128), 1) // 32
    for px in range(2):
        for hx in range(2):
            for hy in range(2):
                for hz in range(2):
                    block = jnp.zeros((64, 128), F32)
                    for py in range(2):
                        for pz in range(2):
                            row = ((px - hx + 1) * 9 + (py - hy + 1) * 3 + (pz - hz + 1)) * 64
                            piece = total[row : row + 64, px * 128 : px * 128 + 128]
                            block = piece if py + pz == 0 else jnp.where(lane == 2 * py + pz, piece, block)
                    at = (px * 8 + hx * 4 + hy * 2 + hz) * 64
                    pay_out[at : at + 64, :] = block


def wgrad_edge_kernel(left, right, cot, pay, keep, give, windows):
    first = first_core()
    fill_windows((0, 5), (None, left, right, None, None, None), windows)
    sums = []
    for px, x in ((0, 0), (1, 3)):
        taps = cot[x, px * 128 : px * 128 + 128, :]
        sums.append(lax.dot_general(windows[px * 576 : px * 576 + 576, :], taps, NT, preferred_element_type=F32))
    lane = lax.broadcasted_iota(jnp.int32, (64, 128), 1) // 32
    for hx in range(2):
        for hy in range(2):
            for hz in range(2):
                at = (hx * 4 + hy * 2 + hz) * 64
                blocks = [pay[at : at + 64, :], pay[512 + at : 512 + at + 64, :]]
                px = 1 - hx
                beyond = jnp.zeros((64, 128), F32)
                for py in range(2):
                    for pz in range(2):
                        row = ((py - hy + 1) * 3 + (pz - hz + 1)) * 64
                        beyond = jnp.where(lane == 2 * py + pz, sums[px][row : row + 64, :], beyond)
                blocks[px] = blocks[px] + beyond
                keep[at : at + 64, :] = jnp.where(first, blocks[0], blocks[1])
                give[at : at + 64, :] = jnp.where(first, blocks[1], blocks[0])


def x_chip():
    return (lax.axis_index("gy") // 8) * 2 + lax.axis_index("gz")


def split_kernel(keep, got, mine, one, two, three):
    for k, out in enumerate((mine, one, two, three)):
        rows = pl.ds(pl.multiple_of((x_chip() ^ k) * 128, 128), 128)
        out[...] = keep[rows, :] + got[rows, :]


def finish_kernel(*refs, factor):
    pieces, (out, taps, sems) = refs[:8], refs[8:]
    copies = []
    core = lax.rem(lax.axis_index("gy"), 2)
    for n in range(8):
        quarter = x_chip() ^ (n % 4)
        px = core if n < 4 else 1 - core
        kx = 2 * (quarter // 2) + 1 - px
        for hz in range(2):
            block = (pieces[n][hz * 64 : hz * 64 + 64, :] * factor).T
            for py in range(2):
                for pz in range(2):
                    spot = (2 * py + pz) * 32
                    taps[kx, 2 * lax.rem(quarter, 2) + 1 - py, 2 * hz + 1 - pz] = block[spot : spot + 32, :]
        two = pl.ds(2 * lax.rem(quarter, 2), 2)
        copies.append(pltpu.make_async_copy(taps.at[kx, two], out.at[kx, two], sems.at[n]))
        copies[-1].start()
    for copy in copies:
        copy.wait()


def up_kernel(own, left, right, low, high, z_all, weight, *rest, start):
    out, windows, matrix, planes, sems = rest[-5:]
    taps = ((3, 1, None), (None, 2, 0))
    fill_windows(range(start, start + 4), (own, left, right, low, high, z_all), windows)
    for px in range(2):
        for py in range(2):
            for pz in range(2):
                pieces = []
                for kx in taps[px]:
                    for ky in taps[py]:
                        for kz in taps[pz]:
                            if kx is None or ky is None or kz is None:
                                pieces.append(jnp.zeros((32, 64), BF16))
                            else:
                                pieces.append(weight[kx, ky, kz])
                row = (px * 4 + py * 2 + pz) * 32
                matrix[row : row + 32, :] = jnp.concatenate(pieces, axis=1)
    copies = []
    for x in range(2):
        result = lax.dot_general(matrix[...], windows[x * 576 : x * 576 + 1728, :], NN, preferred_element_type=F32)
        for n in range(8):
            planes[x, n] = result[n * 32 : n * 32 + 32].reshape(32, 8, 128).astype(BF16)
        copies.append(pltpu.make_async_copy(planes.at[x], out.at[:, :, start + x], sems.at[x]))
        copies[-1].start()
    for copy in copies:
        copy.wait()


def igrad_kernel(own, left, right, low, high, z_all, weight, *rest, start):
    out, windows, matrix, planes, sems = rest[-5:]
    for spot in range(6):
        n = 2 * start + spot
        for ky in range(4):
            py, sy = ((1, -1), (0, 0), (1, 0), (0, 1))[ky]
            plane = cot_plane_of(n, py, own, left, right, low, high, z_all)
            base = spot * 512 + ky * 128
            for y in range(8):
                tile, column = plane(y + sy + 1)
                cells = slice(y * 128, y * 128 + 128)
                windows[base : base + 64, cells] = tile
                windows[base + 64 : base + 96, cells] = rolled(tile[0:32], column, False)
                windows[base + 96 : base + 128, cells] = rolled(tile[32:64], column, True)
    for kx in range(4):
        for ky in range(4):
            row = (kx * 4 + ky) * 128
            for place, kz in enumerate((1, 2, 3, 0)):
                matrix[row + place * 32 : row + place * 32 + 32, :] = weight[kx, ky, kz]
    turned = matrix[...].T
    copies = []
    for x in range(2):
        result = lax.dot_general(turned, windows[x * 1024 : x * 1024 + 2048, :], NN, preferred_element_type=F32)
        planes[x] = result.reshape(64, 8, 128).astype(BF16)
        copies.append(pltpu.make_async_copy(planes.at[x], out.at[:, start + x], sems.at[x]))
        copies[-1].start()
    for copy in copies:
        copy.wait()


def send(block, *flip):
    return lax.ppermute(block, AXES, xor_pairs(*flip))


def beside(block, flip, run, operands):
    block, last = lax.optimization_barrier((block, operands[-1]))
    got = send(block, *flip)
    return lax.optimization_barrier((block, got, run(*operands[:-1], last)))


def body(inputs, weight, cotangent):
    x_up, x_down = ring(4, 1), ring(4, -1)
    swap = [(0, 1), (1, 0)]
    weight_t = weight.transpose(0, 1, 2, 4, 3)

    own, z_face, inner, outer = call(
        prepare_in_kernel,
        (shaped((4, 64, 1024)), shaped((64, 128)), shaped((4, 64, 128)), shaped((4, 64, 128))),
        [pltpu.VMEM((64, 4, 8, 128), BF16), pltpu.SemaphoreType.DMA((4,))],
        far=(0,),
    )(inputs)
    z_own = lax.ppermute(z_face, "gz", swap)
    cot, z_face, inner_cot, outer_cot = call(
        prepare_cot_kernel,
        (shaped((4, 256, 1024)), shaped((128, 128)), shaped((4, 128, 128)), shaped((4, 128, 128))),
        [pltpu.VMEM((8, 32, 4, 8, 128), BF16), pltpu.SemaphoreType.DMA((8,))],
        far=(0,),
    )(cotangent.reshape(8, 32, 4, 8, 128))
    rows = lambda *parts: jnp.concatenate([part.reshape(-1, 128) for part in parts])
    outer = lax.ppermute(rows(outer, z_own, outer_cot), "gy", OUTER)
    inner = lax.ppermute(rows(inner, z_own, inner_cot), "gy", INNER)
    face = shaped((4, 64, 128))
    left, right, low, high, z_all = call(
        side_in_kernel, (shaped((64, 1408)), shaped((64, 1408)), face, face, shaped((64, 128)))
    )(own, z_own, inner, outer)
    left, right, z_face = lax.optimization_barrier((left, right, z_face))
    left, right = lax.ppermute(left, "gx", x_up), lax.ppermute(right, "gx", x_down)
    face = shaped((4, 128, 128))
    cot_left, cot_right, low_cot, high_cot, z_face = call(
        side_cot_kernel, (shaped((128, 1280)), shaped((128, 1280)), face, face, shaped((128, 128)))
    )(cot, z_face, inner, outer)
    z_cot = lax.ppermute(z_face, "gz", swap)
    pay = call(
        wgrad_main_kernel,
        shaped((1024, 128), F32),
        [pltpu.VMEM((2304, 1024), BF16), pltpu.VMEM((1728, 256), F32)],
        flops=2 * 1728 * 256 * 4096,
    )(own, low, high, z_all, cot)
    keep, give = call(
        wgrad_edge_kernel, (shaped((512, 128), F32),) * 2, [pltpu.VMEM((1152, 1024), BF16)], flops=2 * 1152 * 128 * 1024
    )(left, right, cot, pay)
    z_even, z_odd = jnp.tile(z_cot[:64], (2, 1)), jnp.tile(z_cot[64:], (2, 1))
    cot_left, cot_right = jnp.concatenate([cot_left, z_odd], axis=1), jnp.concatenate([cot_right, z_even], axis=1)
    keep, give, cot_left, cot_right = lax.optimization_barrier((keep, give, cot_left, cot_right))
    cot_left = lax.ppermute(cot_left, "gx", x_up)
    cot_right = lax.ppermute(cot_right, "gx", x_down)

    up_shape = jax.ShapeDtypeStruct((8, 32, 4, 8, 128), BF16)
    grad_shape = jax.ShapeDtypeStruct((64, 4, 8, 128), BF16)

    def up_part(start, *into):
        return call(
            functools.partial(up_kernel, start=start),
            up_shape,
            [
                pltpu.VMEM((2304, 1024), BF16),
                pltpu.VMEM((256, 1728), BF16),
                pltpu.VMEM((2, 8, 32, 8, 128), BF16),
                pltpu.SemaphoreType.DMA((2,)),
            ],
            2 * 1728 * 256 * 2048,
            (7,),
            {7: 0} if into else None,
        ), (own, left, right, low, high, z_all, weight_t, *into)

    def igrad_part(start, *into):
        return call(
            functools.partial(igrad_kernel, start=start),
            grad_shape,
            [
                pltpu.VMEM((3072, 1024), BF16),
                pltpu.VMEM((2048, 64), BF16),
                pltpu.VMEM((2, 64, 8, 128), BF16),
                pltpu.SemaphoreType.DMA((2,)),
            ],
            2 * 2048 * 256 * 2048,
            (7,),
            {7: 0} if into else None,
        ), (cot, cot_left, cot_right, low_cot, high_cot, z_cot, weight_t, *into)

    block, one, two, three = call(split_kernel, (shaped((128, 128), F32),) * 4)(keep, send(give, 0, 1, 0))
    along_x = ((0, 0, 1), (0, 8, 0), (0, 8, 1))
    run, operands = up_part(0)
    one, two, three, last = lax.optimization_barrier((one, two, three, operands[-1]))
    got = [send(part, *flip) for part, flip in zip((one, two, three), along_x)]
    block, got, up_0 = lax.optimization_barrier((block, got, run(*operands[:-1], last)))
    block = (block + got[0]) + (got[1] + got[2])
    run, operands = up_part(2, up_0)
    block, got, up = beside(block, (0, 2, 0), run, operands)
    block = block + got
    run, operands = igrad_part(0)
    block, got, grad_0 = beside(block, (0, 6, 0), run, operands)
    block = block + got
    run, operands = igrad_part(2, grad_0)
    block, got, grad = beside(block, (1, 0, 0), run, operands)
    block = block + got
    block = block + send(block, 3, 0, 0)
    mine = [block] + [send(block, *flip) for flip in along_x]
    other = [send(part, 0, 1, 0) for part in mine]
    factor = 1.0 / math.sqrt(4 * 16 * 2 * inputs.shape[1] * inputs.shape[2] * inputs.shape[3])
    weight_grad = call(
        functools.partial(finish_kernel, factor=factor),
        jax.ShapeDtypeStruct((4, 4, 4, 32, 64), F32),
        [pltpu.VMEM((4, 4, 4, 32, 64), F32), pltpu.SemaphoreType.DMA((8,))],
    )(
        *mine, *other
    )
    return up.reshape(2, 2, 2, 32, 4, 8, 128), grad, weight_grad.transpose(0, 1, 2, 4, 3)


def solution(mesh):
    placed = (P(None, "gx", "gy", "gz"), P(), P(None, None, None, None, "gx", "gy", "gz"))
    return jax.shard_map(
        body,
        mesh=mesh,
        in_specs=placed,
        out_specs=(P(None, None, None, None, "gx", "gy", "gz"), P(None, "gx", "gy", "gz"), P()),
        check_vma=False,
    )
```

```python
import functools
import math

import jax
import jax.numpy as jnp
from jax import lax
from jax.experimental import pallas as pl
from jax.experimental.pallas import tpu as pltpu
from jax.sharding import PartitionSpec as P

AXES = ("gx", "gy", "gz")
F32, BF16 = jnp.float32, jnp.bfloat16
NT = (((1,), (1,)), ((), ()))
NN = (((1,), (0,)), ((), ()))
PARAMS = pltpu.CompilerParams(vmem_limit_bytes=24 * 1024 * 1024)
WHOLE = pl.BlockSpec(memory_space=pltpu.VMEM)
FAR = pl.BlockSpec(memory_space=pltpu.HBM)


def shaped(shape, dtype=BF16):
    return pltpu.VMEM(shape, dtype)


def call(kernel, out_shape, scratch=(), flops=0, far=()):
    def run(*operands):
        moved = sum(math.prod(o.shape) * o.dtype.itemsize for o in (*operands, *jax.tree.leaves(out_shape)))
        return pl.pallas_call(
            kernel,
            out_shape=out_shape,
            in_specs=[FAR if n in far else WHOLE for n in range(len(operands))],
            out_specs=jax.tree.map(lambda o: FAR if isinstance(o, jax.ShapeDtypeStruct) else WHOLE, out_shape),
            scratch_shapes=list(scratch),
            compiler_params=PARAMS,
            cost_estimate=pl.CostEstimate(flops=flops, bytes_accessed=moved, transcendentals=0),
        )(*[pltpu.with_memory_space_constraint(o, pltpu.HBM if n in far else pltpu.VMEM) for n, o in enumerate(operands)])

    return run


def rolled(tile, column, before):
    lane = lax.broadcasted_iota(jnp.int32, tile.shape, 1)
    inside = lax.axis_index("gz") == (1 if before else 0)
    edge = jnp.where(inside, column.astype(F32), jnp.zeros(column.shape, F32))
    moved = pltpu.roll(tile, 1 if before else 127, 1).astype(F32)
    return jnp.where(lane == (0 if before else 127), edge, moved).astype(tile.dtype)


def plane_of(xe, own, left, right, low, high, z_all):
    if xe == 0 or xe == 5:
        plane, lane = (left, 1310) if xe == 0 else (right, 1280)
        return lambda ye: (plane[:, ye * 128 : ye * 128 + 128], plane[:, lane + ye : lane + ye + 1])

    def at(ye):
        column = z_all[:, xe * 10 - 10 + ye : xe * 10 - 9 + ye]
        if ye == 0 or ye == 9:
            return (low if ye == 0 else high)[xe - 1], column
        return own[xe - 1, :, ye * 128 - 128 : ye * 128], column

    return at


def xor_pairs(fx, fy, fz):
    pairs = []
    for gx in range(4):
        for gy in range(16):
            for gz in range(2):
                pairs.append(((gx * 16 + gy) * 2 + gz, ((gx ^ fx) * 16 + (gy ^ fy)) * 2 + (gz ^ fz)))
    return pairs


def ring(count, step):
    return [(i, (i + step) % count) for i in range(count)]


OUTER = [(i, (i - 1) % 16 if i % 2 == 0 else (i + 1) % 16) for i in range(16)]
INNER = [(i, i ^ 1) for i in range(16)]


def first_core():
    return lax.rem(lax.axis_index("gy"), 2) == 0


def low_and_high(inner, outer, n):
    a, b, first = inner[n], outer[n], first_core()
    return jnp.where(first, b, a), jnp.where(first, a, b)


def side_picker(x):
    cell = lax.broadcasted_iota(jnp.int32, (1024, 128), 0)
    lane = lax.broadcasted_iota(jnp.int32, (1024, 128), 1)
    side = jnp.where(lax.axis_index("gz") == 0, 127, 0)
    return (cell == (lane - 10 * x - 1) * 128 + side).astype(F32).astype(BF16)


def prepare_in_kernel(raw, own, z_face, inner, outer, arrived, sems):
    copies = [pltpu.make_async_copy(raw.at[16 * n : 16 * n + 16], arrived.at[16 * n : 16 * n + 16], sems.at[n]) for n in range(4)]
    for copy in copies:
        copy.start()
    for n in range(4):
        copies[n].wait()
        for x in range(4):
            own[x, 16 * n : 16 * n + 16, :] = arrived[16 * n : 16 * n + 16, x].reshape(16, 1024)
    faces = jnp.zeros((64, 128), F32)
    for x in range(4):
        plane = own[x]
        low, high = plane[:, 0:128], plane[:, 896:1024]
        inner[x] = jnp.where(first_core(), high, low)
        outer[x] = jnp.where(first_core(), low, high)
        faces += jnp.dot(plane, side_picker(x), preferred_element_type=F32)
    z_face[...] = faces.astype(BF16)


def prepare_cot_kernel(raw, cot, z_face, inner, outer, arrived, sems):
    copies = [pltpu.make_async_copy(raw.at[n], arrived.at[n], sems.at[n]) for n in range(8)]
    for copy in copies:
        copy.start()
    for n in range(8):
        copies[n].wait()
        for x in range(4):
            cot[x, n * 32 : n * 32 + 32, :] = arrived[n, :, x].reshape(32, 1024)
    faces = jnp.zeros((256, 128), F32)
    for x in range(4):
        faces += jnp.dot(cot[x], side_picker(x), preferred_element_type=F32)
        for px in range(2):
            row = px * 128
            low, high = cot[x, row : row + 64, 0:128], cot[x, row + 64 : row + 128, 896:1024]
            inner[x, px * 64 : px * 64 + 64, :] = jnp.where(first_core(), high, low)
            outer[x, px * 64 : px * 64 + 64, :] = jnp.where(first_core(), low, high)
    odd = lax.axis_index("gz") == 0
    for n in range(4):
        even_rows, odd_rows = faces[n * 64 : n * 64 + 32], faces[n * 64 + 32 : n * 64 + 64]
        z_face[n * 32 : n * 32 + 32, :] = jnp.where(odd, odd_rows, even_rows).astype(BF16)


def side_in_kernel(own, z_own, inner, outer, up, down, low, high, z_all):
    lane = lax.broadcasted_iota(jnp.int32, (64, 128), 1)
    z_low, z_high = (tile.astype(F32) for tile in low_and_high(inner, outer, slice(256, 320)))
    every = z_own[...].astype(F32)
    for x in range(4):
        low[x], high[x] = low_and_high(inner, outer, slice(x * 64, x * 64 + 64))
        every = jnp.where(lane == x * 10, z_low[:, x * 10 + 8 : x * 10 + 9], every)
        every = jnp.where(lane == x * 10 + 9, z_high[:, x * 10 + 1 : x * 10 + 2], every)
    z_all[...] = every.astype(BF16)
    for x, out in ((0, down), (3, up)):
        out[:, 0:128] = low[x]
        out[:, 128:1152] = own[x]
        out[:, 1152:1280] = high[x]
        out[:, 1280:1408] = z_all[...]


def side_cot_kernel(z_face, inner, outer, low, high, z_out):
    lane = lax.broadcasted_iota(jnp.int32, (32, 128), 1)
    odd = lax.axis_index("gz") == 0
    for x in range(4):
        low[x], high[x] = low_and_high(inner, outer, slice(320 + x * 128, 448 + x * 128))
    for px in range(2):
        for py, side, spot in ((0, high, 9), (1, low, 0)):
            rows = slice((px * 2 + py) * 32, (px * 2 + py) * 32 + 32)
            face = z_face[rows, :].astype(F32)
            for x in range(4):
                even_rows, odd_rows = side[x, px * 64 : px * 64 + 32, :], side[x, px * 64 + 32 : px * 64 + 64, :]
                column = jnp.where(odd, odd_rows[:, 127:128].astype(F32), even_rows[:, 0:1].astype(F32))
                face = jnp.where(lane == x * 10 + spot, column, face)
            z_out[rows, :] = face.astype(BF16)


def sides_cot_kernel(cot, low, high, z_all, up, down):
    nothing = jnp.zeros((64, 128), BF16)
    for x, px, out in ((0, 0, down), (3, 1, up)):
        out[0:64, 0:128] = nothing
        out[64:128, 0:128] = low[x, px * 64 : px * 64 + 64, :]
        out[:, 128:1152] = cot[x, px * 128 : px * 128 + 128, :]
        out[0:64, 1152:1280] = high[x, px * 64 : px * 64 + 64, :]
        out[64:128, 1152:1280] = nothing
        out[0:64, 1280:1408] = z_all[px * 64 : px * 64 + 64, :]
        out[64:128, 1280:1408] = nothing


def cot_plane_of(n, py, own, left, right, low, high, z_all):
    xe, px = (n + 1) // 2, (n + 1) % 2
    if xe == 0 or xe == 5:
        part, lane = (left, 1310) if xe == 0 else (right, 1280)
        rows, halo = slice(py * 64, py * 64 + 64), slice(py * 32, py * 32 + 32)
        return lambda ye: (part[rows, ye * 128 : ye * 128 + 128], part[halo, lane + ye : lane + ye + 1])

    def at(ye):
        row = (px * 2 + py) * 32
        column = z_all[row : row + 32, xe * 10 - 10 + ye : xe * 10 - 9 + ye]
        if ye == 0 or ye == 9:
            return (low if ye == 0 else high)[xe - 1, px * 64 : px * 64 + 64, :], column
        row = px * 128 + py * 64
        return own[xe - 1, row : row + 64, ye * 128 - 128 : ye * 128], column

    return at


def fill_windows(planes, block, windows):
    for spot, xe in enumerate(planes):
        plane = plane_of(xe, *block)
        for ye in range(10):
            tile, column = plane(ye)
            three = (rolled(tile, column, True), tile, rolled(tile, column, False))
            for sy in range(3):
                at = ye - sy
                if 0 <= at < 8:
                    for sz in range(3):
                        row = spot * 576 + sy * 192 + sz * 64
                        windows[row : row + 64, at * 128 : at * 128 + 128] = three[sz]


def wgrad_main_kernel(own, low, high, z_all, cot, pay_out, windows, total):
    fill_windows(range(1, 5), (own, None, None, low, high, z_all), windows)
    for x in (1, 0, 2, 3):
        first, last = max(x - 1, 0), min(x + 1, 3)
        part = lax.dot_general(windows[first * 576 : last * 576 + 576, :], cot[x], NT, preferred_element_type=F32)
        if x == 1:
            total[...] = part
        else:
            row = (first - x + 1) * 576
            total[row : row + part.shape[0], :] += part
    lane = lax.broadcasted_iota(jnp.int32, (64, 128), 1) // 32
    for px in range(2):
        for hx in range(2):
            for hy in range(2):
                for hz in range(2):
                    block = jnp.zeros((64, 128), F32)
                    for py in range(2):
                        for pz in range(2):
                            row = ((px - hx + 1) * 9 + (py - hy + 1) * 3 + (pz - hz + 1)) * 64
                            piece = total[row : row + 64, px * 128 : px * 128 + 128]
                            block = piece if py + pz == 0 else jnp.where(lane == 2 * py + pz, piece, block)
                    at = (px * 8 + hx * 4 + hy * 2 + hz) * 64
                    pay_out[at : at + 64, :] = block


def wgrad_edge_kernel(left, right, cot, pay, keep, give, windows):
    first = first_core()
    fill_windows((0, 5), (None, left, right, None, None, None), windows)
    sums = []
    for px, x in ((0, 0), (1, 3)):
        taps = cot[x, px * 128 : px * 128 + 128, :]
        sums.append(lax.dot_general(windows[px * 576 : px * 576 + 576, :], taps, NT, preferred_element_type=F32))
    lane = lax.broadcasted_iota(jnp.int32, (64, 128), 1) // 32
    for hx in range(2):
        for hy in range(2):
            for hz in range(2):
                at = (hx * 4 + hy * 2 + hz) * 64
                blocks = [pay[at : at + 64, :], pay[512 + at : 512 + at + 64, :]]
                px = 1 - hx
                beyond = jnp.zeros((64, 128), F32)
                for py in range(2):
                    for pz in range(2):
                        row = ((py - hy + 1) * 3 + (pz - hz + 1)) * 64
                        beyond = jnp.where(lane == 2 * py + pz, sums[px][row : row + 64, :], beyond)
                blocks[px] = blocks[px] + beyond
                keep[at : at + 64, :] = jnp.where(first, blocks[0], blocks[1])
                give[at : at + 64, :] = jnp.where(first, blocks[1], blocks[0])


def x_chip():
    return (lax.axis_index("gy") // 8) * 2 + lax.axis_index("gz")


def split_kernel(keep, got, mine, one, two, three):
    for k, out in enumerate((mine, one, two, three)):
        rows = pl.ds(pl.multiple_of((x_chip() ^ k) * 128, 128), 128)
        out[...] = keep[rows, :] + got[rows, :]


def finish_kernel(*refs, factor):
    pieces, (out, taps, sems) = refs[:8], refs[8:]
    copies = []
    core = lax.rem(lax.axis_index("gy"), 2)
    for n in range(8):
        quarter = x_chip() ^ (n % 4)
        px = core if n < 4 else 1 - core
        kx = 2 * (quarter // 2) + 1 - px
        for hz in range(2):
            block = (pieces[n][hz * 64 : hz * 64 + 64, :] * factor).T
            for py in range(2):
                for pz in range(2):
                    spot = (2 * py + pz) * 32
                    taps[kx, 2 * lax.rem(quarter, 2) + 1 - py, 2 * hz + 1 - pz] = block[spot : spot + 32, :]
        two = pl.ds(2 * lax.rem(quarter, 2), 2)
        copies.append(pltpu.make_async_copy(taps.at[kx, two], out.at[kx, two], sems.at[n]))
        copies[-1].start()
    for copy in copies:
        copy.wait()


def weights_kernel(weight, for_up, for_grad, turned):
    taps = ((3, 1, None), (None, 2, 0))
    for px in range(2):
        for py in range(2):
            for pz in range(2):
                pieces = []
                for kx in taps[px]:
                    for ky in taps[py]:
                        for kz in taps[pz]:
                            if kx is None or ky is None or kz is None:
                                pieces.append(jnp.zeros((32, 64), BF16))
                            else:
                                pieces.append(weight[kx, ky, kz])
                row = (px * 4 + py * 2 + pz) * 32
                for_up[row : row + 32, :] = jnp.concatenate(pieces, axis=1)
    for kx in range(4):
        for ky in range(4):
            row = (kx * 4 + ky) * 128
            for place, kz in enumerate((1, 2, 3, 0)):
                turned[row + place * 32 : row + place * 32 + 32, :] = weight[kx, ky, kz]
    for_grad[...] = turned[...].T


def up_kernel(own, left, right, low, high, z_all, matrix, out, windows, planes, sems):
    fill_windows(range(6), (own, left, right, low, high, z_all), windows)
    copies = []
    for x in range(4):
        result = lax.dot_general(matrix[...], windows[x * 576 : x * 576 + 1728, :], NN, preferred_element_type=F32)
        for n in range(8):
            part = result[n * 32 : n * 32 + 32].astype(BF16)
            part = jnp.stack([part[:, y * 128 : y * 128 + 128] for y in range(8)], 0)
            planes[x, n] = jnp.swapaxes(part, 0, 1)
            copies.append(pltpu.make_async_copy(planes.at[x, n], out.at[n, :, x], sems.at[x, n]))
            copies[-1].start()
    for copy in copies:
        copy.wait()


def igrad_kernel(own, left, right, low, high, z_all, matrix, out, windows, planes, sems):
    for n in range(10):
        for ky in range(4):
            py, sy = ((1, -1), (0, 0), (1, 0), (0, 1))[ky]
            plane = cot_plane_of(n, py, own, left, right, low, high, z_all)
            base = n * 512 + ky * 128
            for y in range(8):
                tile, column = plane(y + sy + 1)
                cells = slice(y * 128, y * 128 + 128)
                windows[base : base + 64, cells] = tile
                windows[base + 64 : base + 96, cells] = rolled(tile[0:32], column, False)
                windows[base + 96 : base + 128, cells] = rolled(tile[32:64], column, True)
    copies = []
    for x in range(4):
        result = lax.dot_general(matrix[...], windows[x * 1024 : x * 1024 + 2048, :], NN, preferred_element_type=F32)
        planes[x] = result.reshape(64, 8, 128).astype(BF16)
        copies.append(pltpu.make_async_copy(planes.at[x], out.at[:, x], sems.at[x]))
        copies[-1].start()
    for copy in copies:
        copy.wait()


def send(block, *flip):
    return lax.ppermute(block, AXES, xor_pairs(*flip))


def beside(parts, flips, *works):
    parts, last = lax.optimization_barrier((parts, [operands[-1] for _, operands in works]))
    got = [send(part, *flip) for part, flip in zip(parts, flips)]
    done = [run(*operands[:-1], carry) for (run, operands), carry in zip(works, last)]
    return lax.optimization_barrier((parts, got, done))


def body(inputs, weight, cotangent):
    x_up, x_down = ring(4, 1), ring(4, -1)
    swap = [(0, 1), (1, 0)]
    weight_t = weight.transpose(0, 1, 2, 4, 3)

    own, z_face, inner, outer = call(
        prepare_in_kernel,
        (shaped((4, 64, 1024)), shaped((64, 128)), shaped((4, 64, 128)), shaped((4, 64, 128))),
        [pltpu.VMEM((64, 4, 8, 128), BF16), pltpu.SemaphoreType.DMA((4,))],
        far=(0,),
    )(inputs)
    z_own = lax.ppermute(z_face, "gz", swap)
    cot, z_face, inner_cot, outer_cot = call(
        prepare_cot_kernel,
        (shaped((4, 256, 1024)), shaped((128, 128)), shaped((4, 128, 128)), shaped((4, 128, 128))),
        [pltpu.VMEM((8, 32, 4, 8, 128), BF16), pltpu.SemaphoreType.DMA((8,))],
        far=(0,),
    )(cotangent.reshape(8, 32, 4, 8, 128))
    rows = lambda *parts: jnp.concatenate([part.reshape(-1, 128) for part in parts])
    z_own, weight_t = lax.optimization_barrier((z_own, weight_t))
    for_up, for_grad = call(
        weights_kernel, (shaped((256, 1728)), shaped((64, 2048))), [pltpu.VMEM((2048, 64), BF16)], far=()
    )(weight_t)
    outer = lax.ppermute(rows(outer, z_own, outer_cot), "gy", OUTER)
    inner = lax.ppermute(rows(inner, z_own, inner_cot), "gy", INNER)
    inner, outer, for_up, for_grad = lax.optimization_barrier((inner, outer, for_up, for_grad))
    face = shaped((4, 64, 128))
    left, right, low, high, z_all = call(
        side_in_kernel, (shaped((64, 1408)), shaped((64, 1408)), face, face, shaped((64, 128)))
    )(own, z_own, inner, outer)
    left, right, z_face = lax.optimization_barrier((left, right, z_face))
    left, right = lax.ppermute(left, "gx", x_up), lax.ppermute(right, "gx", x_down)
    face = shaped((4, 128, 128))
    low_cot, high_cot, z_face = call(side_cot_kernel, (face, face, shaped((128, 128))))(z_face, inner, outer)
    z_cot = lax.ppermute(z_face, "gz", swap)
    pay = call(
        wgrad_main_kernel,
        shaped((1024, 128), F32),
        [pltpu.VMEM((2304, 1024), BF16), pltpu.VMEM((1728, 256), F32)],
        flops=2 * 1728 * 256 * 4096,
    )(own, low, high, z_all, cot)
    left, right, z_cot = lax.optimization_barrier((left, right, z_cot))
    keep, give = call(
        wgrad_edge_kernel, (shaped((512, 128), F32),) * 2, [pltpu.VMEM((1152, 1024), BF16)], flops=2 * 1152 * 128 * 1024
    )(left, right, cot, pay)
    up_work = call(
        up_kernel,
        jax.ShapeDtypeStruct((8, 32, 4, 8, 128), BF16),
        [pltpu.VMEM((3456, 1024), BF16), pltpu.VMEM((4, 8, 32, 8, 128), BF16), pltpu.SemaphoreType.DMA((4, 8))],
        flops=2 * 1728 * 256 * 4096,
    ), (own, left, right, low, high, z_all, for_up)
    grad_work = call(
        igrad_kernel,
        jax.ShapeDtypeStruct((64, 4, 8, 128), BF16),
        [pltpu.VMEM((5120, 1024), BF16), pltpu.VMEM((4, 64, 8, 128), BF16), pltpu.SemaphoreType.DMA((4,))],
        flops=2 * 2048 * 256 * 4096,
    )

    block, one, two, three = call(split_kernel, (shaped((128, 128), F32),) * 4)(keep, send(give, 0, 1, 0))
    along_x = ((0, 0, 1), (0, 8, 0), (0, 8, 1))
    (one, two, three), last = lax.optimization_barrier(((one, two, three), z_cot))
    got = [send(part, *flip) for part, flip in zip((one, two, three), along_x)]
    cot_left, cot_right = call(sides_cot_kernel, (shaped((128, 1408)), shaped((128, 1408))), flops=2 * 1728 * 256 * 2048)(
        cot, low_cot, high_cot, last
    )
    cot_left, cot_right = lax.ppermute(cot_left, "gx", x_up), lax.ppermute(cot_right, "gx", x_down)
    block = (block + got[0]) + (got[1] + got[2])
    along_y, along_z = ((1, 0, 0), (2, 0, 0), (3, 0, 0)), ((0, 2, 0), (0, 4, 0), (0, 6, 0))
    (block, *_), got, (up,) = beside([block] * 3, along_z, up_work)
    block = (block + got[0]) + (got[1] + got[2])
    grad_work = grad_work, (cot, cot_left, cot_right, low_cot, high_cot, z_cot, for_grad)
    (block, *_), got, (grad,) = beside([block] * 3, along_y, grad_work)
    block = (block + got[0]) + (got[1] + got[2])
    mine = [block] + [send(block, *flip) for flip in along_x]
    other = [send(part, 0, 1, 0) for part in mine]
    factor = 1.0 / math.sqrt(4 * 16 * 2 * inputs.shape[1] * inputs.shape[2] * inputs.shape[3])
    weight_grad = call(
        functools.partial(finish_kernel, factor=factor),
        jax.ShapeDtypeStruct((4, 4, 4, 32, 64), F32),
        [pltpu.VMEM((4, 4, 4, 32, 64), F32), pltpu.SemaphoreType.DMA((8,))],
    )(
        *mine, *other
    )
    return up.reshape(2, 2, 2, 32, 4, 8, 128), grad, weight_grad.transpose(0, 1, 2, 4, 3)


def solution(mesh):
    placed = (P(None, "gx", "gy", "gz"), P(), P(None, None, None, None, "gx", "gy", "gz"))
    return jax.shard_map(
        body,
        mesh=mesh,
        in_specs=placed,
        out_specs=(P(None, None, None, None, "gx", "gy", "gz"), P(None, "gx", "gy", "gz"), P()),
        check_vma=False,
    )
```

```python
import functools
import math

import jax
import jax.numpy as jnp
from jax import lax
from jax.experimental import pallas as pl
from jax.experimental.pallas import tpu as pltpu
from jax.sharding import PartitionSpec as P

AXES = ("gx", "gy", "gz")
F32, BF16 = jnp.float32, jnp.bfloat16
NT = (((1,), (1,)), ((), ()))
NN = (((1,), (0,)), ((), ()))
PARAMS = pltpu.CompilerParams(vmem_limit_bytes=24 * 1024 * 1024)
WHOLE = pl.BlockSpec(memory_space=pltpu.VMEM)
FAR = pl.BlockSpec(memory_space=pltpu.HBM)


def shaped(shape, dtype=BF16):
    return pltpu.VMEM(shape, dtype)


def call(kernel, out_shape, scratch=(), flops=0, far=(), aliases=None):
    def run(*operands):
        moved = sum(math.prod(o.shape) * o.dtype.itemsize for o in (*operands, *jax.tree.leaves(out_shape)))
        return pl.pallas_call(
            kernel,
            out_shape=out_shape,
            in_specs=[FAR if n in far else WHOLE for n in range(len(operands))],
            out_specs=jax.tree.map(lambda o: FAR if isinstance(o, jax.ShapeDtypeStruct) else WHOLE, out_shape),
            scratch_shapes=list(scratch),
            compiler_params=PARAMS,
            input_output_aliases=aliases or {},
            cost_estimate=pl.CostEstimate(flops=flops, bytes_accessed=moved, transcendentals=0),
        )(*[pltpu.with_memory_space_constraint(o, pltpu.HBM if n in far else pltpu.VMEM) for n, o in enumerate(operands)])

    return run


def rolled(tile, column, before):
    lane = lax.broadcasted_iota(jnp.int32, tile.shape, 1)
    inside = lax.axis_index("gz") == (1 if before else 0)
    edge = jnp.where(inside, column.astype(F32), jnp.zeros(column.shape, F32))
    moved = pltpu.roll(tile, 1 if before else 127, 1).astype(F32)
    return jnp.where(lane == (0 if before else 127), edge, moved).astype(tile.dtype)


def plane_of(xe, own, left, right, low, high, z_all):
    if xe == 0 or xe == 5:
        plane, lane = (left, 1310) if xe == 0 else (right, 1280)
        return lambda ye: (plane[:, ye * 128 : ye * 128 + 128], plane[:, lane + ye : lane + ye + 1])

    def at(ye):
        column = z_all[:, xe * 10 - 10 + ye : xe * 10 - 9 + ye]
        if ye == 0 or ye == 9:
            return (low if ye == 0 else high)[xe - 1], column
        return own[xe - 1, :, ye * 128 - 128 : ye * 128], column

    return at


def xor_pairs(fx, fy, fz):
    pairs = []
    for gx in range(4):
        for gy in range(16):
            for gz in range(2):
                pairs.append(((gx * 16 + gy) * 2 + gz, ((gx ^ fx) * 16 + (gy ^ fy)) * 2 + (gz ^ fz)))
    return pairs


def ring(count, step):
    return [(i, (i + step) % count) for i in range(count)]


OUTER = [(i, (i - 1) % 16 if i % 2 == 0 else (i + 1) % 16) for i in range(16)]
INNER = [(i, i ^ 1) for i in range(16)]


def first_core():
    return lax.rem(lax.axis_index("gy"), 2) == 0


def low_and_high(inner, outer, n):
    a, b, first = inner[n], outer[n], first_core()
    return jnp.where(first, b, a), jnp.where(first, a, b)


def side_picker(x):
    cell = lax.broadcasted_iota(jnp.int32, (1024, 128), 0)
    lane = lax.broadcasted_iota(jnp.int32, (1024, 128), 1)
    side = jnp.where(lax.axis_index("gz") == 0, 127, 0)
    return (cell == (lane - 10 * x - 1) * 128 + side).astype(F32).astype(BF16)


def prepare_in_kernel(raw, own, z_face, inner, outer, arrived, sems):
    copies = [pltpu.make_async_copy(raw.at[16 * n : 16 * n + 16], arrived.at[16 * n : 16 * n + 16], sems.at[n]) for n in range(4)]
    for copy in copies:
        copy.start()
    for n in range(4):
        copies[n].wait()
        for x in range(4):
            own[x, 16 * n : 16 * n + 16, :] = arrived[16 * n : 16 * n + 16, x].reshape(16, 1024)
    faces = jnp.zeros((64, 128), F32)
    for x in range(4):
        plane = own[x]
        low, high = plane[:, 0:128], plane[:, 896:1024]
        inner[x] = jnp.where(first_core(), high, low)
        outer[x] = jnp.where(first_core(), low, high)
        faces += jnp.dot(plane, side_picker(x), preferred_element_type=F32)
    z_face[...] = faces.astype(BF16)


def prepare_cot_kernel(raw, cot, z_face, inner, outer, arrived, sems):
    copies = [pltpu.make_async_copy(raw.at[n], arrived.at[n], sems.at[n]) for n in range(8)]
    for copy in copies:
        copy.start()
    for n in range(8):
        copies[n].wait()
        for x in range(4):
            cot[x, n * 32 : n * 32 + 32, :] = arrived[n, :, x].reshape(32, 1024)
    faces = jnp.zeros((256, 128), F32)
    for x in range(4):
        faces += jnp.dot(cot[x], side_picker(x), preferred_element_type=F32)
        for px in range(2):
            row = px * 128
            low, high = cot[x, row : row + 64, 0:128], cot[x, row + 64 : row + 128, 896:1024]
            inner[x, px * 64 : px * 64 + 64, :] = jnp.where(first_core(), high, low)
            outer[x, px * 64 : px * 64 + 64, :] = jnp.where(first_core(), low, high)
    odd = lax.axis_index("gz") == 0
    for n in range(4):
        even_rows, odd_rows = faces[n * 64 : n * 64 + 32], faces[n * 64 + 32 : n * 64 + 64]
        z_face[n * 32 : n * 32 + 32, :] = jnp.where(odd, odd_rows, even_rows).astype(BF16)


def side_in_kernel(own, z_own, inner, outer, up, down, low, high, z_all):
    lane = lax.broadcasted_iota(jnp.int32, (64, 128), 1)
    z_low, z_high = (tile.astype(F32) for tile in low_and_high(inner, outer, slice(256, 320)))
    every = z_own[...].astype(F32)
    for x in range(4):
        low[x], high[x] = low_and_high(inner, outer, slice(x * 64, x * 64 + 64))
        every = jnp.where(lane == x * 10, z_low[:, x * 10 + 8 : x * 10 + 9], every)
        every = jnp.where(lane == x * 10 + 9, z_high[:, x * 10 + 1 : x * 10 + 2], every)
    z_all[...] = every.astype(BF16)
    for x, out in ((0, down), (3, up)):
        out[:, 0:128] = low[x]
        out[:, 128:1152] = own[x]
        out[:, 1152:1280] = high[x]
        out[:, 1280:1408] = z_all[...]


def side_cot_kernel(z_face, inner, outer, low, high, z_out):
    lane = lax.broadcasted_iota(jnp.int32, (32, 128), 1)
    odd = lax.axis_index("gz") == 0
    for x in range(4):
        low[x], high[x] = low_and_high(inner, outer, slice(320 + x * 128, 448 + x * 128))
    for px in range(2):
        for py, side, spot in ((0, high, 9), (1, low, 0)):
            rows = slice((px * 2 + py) * 32, (px * 2 + py) * 32 + 32)
            face = z_face[rows, :].astype(F32)
            for x in range(4):
                even_rows, odd_rows = side[x, px * 64 : px * 64 + 32, :], side[x, px * 64 + 32 : px * 64 + 64, :]
                column = jnp.where(odd, odd_rows[:, 127:128].astype(F32), even_rows[:, 0:1].astype(F32))
                face = jnp.where(lane == x * 10 + spot, column, face)
            z_out[rows, :] = face.astype(BF16)


def sides_cot_kernel(cot, low, high, z_all, up, down):
    nothing = jnp.zeros((64, 128), BF16)
    for x, px, out in ((0, 0, down), (3, 1, up)):
        out[0:64, 0:128] = nothing
        out[64:128, 0:128] = low[x, px * 64 : px * 64 + 64, :]
        out[:, 128:1152] = cot[x, px * 128 : px * 128 + 128, :]
        out[0:64, 1152:1280] = high[x, px * 64 : px * 64 + 64, :]
        out[64:128, 1152:1280] = nothing
        out[0:64, 1280:1408] = z_all[px * 64 : px * 64 + 64, :]
        out[64:128, 1280:1408] = nothing


def cot_plane_of(n, py, own, left, right, low, high, z_all):
    xe, px = (n + 1) // 2, (n + 1) % 2
    if xe == 0 or xe == 5:
        part, lane = (left, 1310) if xe == 0 else (right, 1280)
        rows, halo = slice(py * 64, py * 64 + 64), slice(py * 32, py * 32 + 32)
        return lambda ye: (part[rows, ye * 128 : ye * 128 + 128], part[halo, lane + ye : lane + ye + 1])

    def at(ye):
        row = (px * 2 + py) * 32
        column = z_all[row : row + 32, xe * 10 - 10 + ye : xe * 10 - 9 + ye]
        if ye == 0 or ye == 9:
            return (low if ye == 0 else high)[xe - 1, px * 64 : px * 64 + 64, :], column
        row = px * 128 + py * 64
        return own[xe - 1, row : row + 64, ye * 128 - 128 : ye * 128], column

    return at


def fill_windows(planes, block, windows, y_halo=True):
    for spot, xe in enumerate(planes):
        plane = plane_of(xe, *block)
        if not y_halo:
            windows[spot * 576 : spot * 576 + 192, 0:128] = jnp.zeros((192, 128), BF16)
            windows[spot * 576 + 384 : spot * 576 + 576, 896:1024] = jnp.zeros((192, 128), BF16)
        for ye in range(10) if y_halo else range(1, 9):
            tile, column = plane(ye)
            three = (rolled(tile, column, True), tile, rolled(tile, column, False))
            for sy in range(3):
                at = ye - sy
                if 0 <= at < 8:
                    for sz in range(3):
                        row = spot * 576 + sy * 192 + sz * 64
                        windows[row : row + 64, at * 128 : at * 128 + 128] = three[sz]


def wgrad_main_kernel(own, z_own, cot, pay_out, windows, total):
    fill_windows(range(1, 5), (own, None, None, None, None, z_own), windows, False)
    for x in (1, 0, 2, 3):
        first, last = max(x - 1, 0), min(x + 1, 3)
        part = lax.dot_general(windows[first * 576 : last * 576 + 576, :], cot[x], NT, preferred_element_type=F32)
        if x == 1:
            total[...] = part
        else:
            row = (first - x + 1) * 576
            total[row : row + part.shape[0], :] += part
    lane = lax.broadcasted_iota(jnp.int32, (64, 128), 1) // 32
    for px in range(2):
        for hx in range(2):
            for hy in range(2):
                for hz in range(2):
                    block = jnp.zeros((64, 128), F32)
                    for py in range(2):
                        for pz in range(2):
                            row = ((px - hx + 1) * 9 + (py - hy + 1) * 3 + (pz - hz + 1)) * 64
                            piece = total[row : row + 64, px * 128 : px * 128 + 128]
                            block = piece if py + pz == 0 else jnp.where(lane == 2 * py + pz, piece, block)
                    at = (px * 8 + hx * 4 + hy * 2 + hz) * 64
                    pay_out[at : at + 64, :] = block


def wgrad_y_kernel(low, high, z_all, cot, pay, pay_out, windows, totals):
    for edge, (side, ye) in enumerate(((low, 0), (high, 9))):
        for x in range(4):
            tile, column = side[x], z_all[:, x * 10 + ye : x * 10 + ye + 1]
            windows[x * 192 : x * 192 + 64, :] = rolled(tile, column, True)
            windows[x * 192 + 64 : x * 192 + 128, :] = tile
            windows[x * 192 + 128 : x * 192 + 192, :] = rolled(tile, column, False)
        cells = slice(0, 128) if edge == 0 else slice(896, 1024)
        for x in (1, 0, 2, 3):
            first, last = max(x - 1, 0), min(x + 1, 3)
            part = lax.dot_general(
                windows[first * 192 : last * 192 + 192, :], cot[x, :, cells], NT, preferred_element_type=F32
            )
            row = (first - x + 1) * 192
            if x == 1:
                totals[edge] = part
            else:
                totals[edge, row : row + part.shape[0], :] += part
    lane = lax.broadcasted_iota(jnp.int32, (64, 128), 1) // 32
    for px in range(2):
        for hx in range(2):
            for hy in range(2):
                for hz in range(2):
                    at = (px * 8 + hx * 4 + hy * 2 + hz) * 64
                    block = pay[at : at + 64, :]
                    py = 1 - hy
                    for pz in range(2):
                        row = ((px - hx + 1) * 3 + (pz - hz + 1)) * 64
                        piece = totals[0 if py - hy < 0 else 1, row : row + 64, px * 128 : px * 128 + 128]
                        block = jnp.where(lane == 2 * py + pz, block + piece, block)
                    pay_out[at : at + 64, :] = block


def wgrad_edge_kernel(left, right, cot, pay, keep, give, windows):
    first = first_core()
    fill_windows((0, 5), (None, left, right, None, None, None), windows)
    sums = []
    for px, x in ((0, 0), (1, 3)):
        taps = cot[x, px * 128 : px * 128 + 128, :]
        sums.append(lax.dot_general(windows[px * 576 : px * 576 + 576, :], taps, NT, preferred_element_type=F32))
    lane = lax.broadcasted_iota(jnp.int32, (64, 128), 1) // 32
    for hx in range(2):
        for hy in range(2):
            for hz in range(2):
                at = (hx * 4 + hy * 2 + hz) * 64
                blocks = [pay[at : at + 64, :], pay[512 + at : 512 + at + 64, :]]
                px = 1 - hx
                beyond = jnp.zeros((64, 128), F32)
                for py in range(2):
                    for pz in range(2):
                        row = ((py - hy + 1) * 3 + (pz - hz + 1)) * 64
                        beyond = jnp.where(lane == 2 * py + pz, sums[px][row : row + 64, :], beyond)
                blocks[px] = blocks[px] + beyond
                keep[at : at + 64, :] = jnp.where(first, blocks[0], blocks[1])
                give[at : at + 64, :] = jnp.where(first, blocks[1], blocks[0])


def x_chip():
    return (lax.axis_index("gy") // 8) * 2 + lax.axis_index("gz")


def split_kernel(keep, got, mine, one, two, three):
    for k, out in enumerate((mine, one, two, three)):
        rows = pl.ds(pl.multiple_of((x_chip() ^ k) * 128, 128), 128)
        out[...] = keep[rows, :] + got[rows, :]


def finish_kernel(*refs, factor):
    pieces, (out, taps, sems) = refs[:8], refs[8:]
    copies = []
    core = lax.rem(lax.axis_index("gy"), 2)
    for n in range(8):
        quarter = x_chip() ^ (n % 4)
        px = core if n < 4 else 1 - core
        kx = 2 * (quarter // 2) + 1 - px
        for hz in range(2):
            block = (pieces[n][hz * 64 : hz * 64 + 64, :] * factor).T
            for py in range(2):
                for pz in range(2):
                    spot = (2 * py + pz) * 32
                    taps[kx, 2 * lax.rem(quarter, 2) + 1 - py, 2 * hz + 1 - pz] = block[spot : spot + 32, :]
        two = pl.ds(2 * lax.rem(quarter, 2), 2)
        copies.append(pltpu.make_async_copy(taps.at[kx, two], out.at[kx, two], sems.at[n]))
        copies[-1].start()
    for copy in copies:
        copy.wait()


def weights_kernel(weight, for_up, for_grad, turned):
    taps = ((3, 1, None), (None, 2, 0))
    for px in range(2):
        for py in range(2):
            for pz in range(2):
                pieces = []
                for kx in taps[px]:
                    for ky in taps[py]:
                        for kz in taps[pz]:
                            if kx is None or ky is None or kz is None:
                                pieces.append(jnp.zeros((32, 64), BF16))
                            else:
                                pieces.append(weight[kx, ky, kz])
                row = (px * 4 + py * 2 + pz) * 32
                for_up[row : row + 32, :] = jnp.concatenate(pieces, axis=1)
    for kx in range(4):
        for ky in range(4):
            row = (kx * 4 + ky) * 128
            for place, kz in enumerate((1, 2, 3, 0)):
                turned[row + place * 32 : row + place * 32 + 32, :] = weight[kx, ky, kz]
    for_grad[...] = turned[...].T


def up_inside_kernel(own, low, high, z_all, *rest):
    up_planes((1, 2), 1, (own, None, None, low, high, z_all), *rest)


def up_outside_kernel(own, left, right, low, high, z_all, inside, *rest):
    up_planes((0, 3), 0, (own, left, right, low, high, z_all), *rest)


def up_planes(wanted, start, block, matrix, out, windows, planes, sems):
    fill_windows(range(start, 6 - start), block, windows)
    copies = []
    for spot, x in enumerate(wanted):
        row = (x - start) * 576
        result = lax.dot_general(matrix[...], windows[row : row + 1728, :], NN, preferred_element_type=F32)
        for n in range(8):
            part = result[n * 32 : n * 32 + 32].astype(BF16)
            part = jnp.stack([part[:, y * 128 : y * 128 + 128] for y in range(8)], 0)
            planes[spot, n] = jnp.swapaxes(part, 0, 1)
            copies.append(pltpu.make_async_copy(planes.at[spot, n], out.at[n, :, x], sems.at[spot, n]))
            copies[-1].start()
    for copy in copies:
        copy.wait()


def igrad_kernel(own, left, right, low, high, z_all, matrix, out, windows, planes, sems):
    for n in range(10):
        for ky in range(4):
            py, sy = ((1, -1), (0, 0), (1, 0), (0, 1))[ky]
            plane = cot_plane_of(n, py, own, left, right, low, high, z_all)
            base = n * 512 + ky * 128
            for y in range(8):
                tile, column = plane(y + sy + 1)
                cells = slice(y * 128, y * 128 + 128)
                windows[base : base + 64, cells] = tile
                windows[base + 64 : base + 96, cells] = rolled(tile[0:32], column, False)
                windows[base + 96 : base + 128, cells] = rolled(tile[32:64], column, True)
    copies = []
    for x in range(4):
        result = lax.dot_general(matrix[...], windows[x * 1024 : x * 1024 + 2048, :], NN, preferred_element_type=F32)
        planes[x] = result.reshape(64, 8, 128).astype(BF16)
        copies.append(pltpu.make_async_copy(planes.at[x], out.at[:, x], sems.at[x]))
        copies[-1].start()
    for copy in copies:
        copy.wait()


def send(block, *flip):
    return lax.ppermute(block, AXES, xor_pairs(*flip))


def beside(parts, flips, *works):
    parts, last = lax.optimization_barrier((parts, [operands[-1] for _, operands in works]))
    got = [send(part, *flip) for part, flip in zip(parts, flips)]
    done = [run(*operands[:-1], carry) for (run, operands), carry in zip(works, last)]
    return lax.optimization_barrier((parts, got, done))


def body(inputs, weight, cotangent):
    x_up, x_down = ring(4, 1), ring(4, -1)
    swap = [(0, 1), (1, 0)]
    weight_t = weight.transpose(0, 1, 2, 4, 3)

    own, z_face, inner, outer = call(
        prepare_in_kernel,
        (shaped((4, 64, 1024)), shaped((64, 128)), shaped((4, 64, 128)), shaped((4, 64, 128))),
        [pltpu.VMEM((64, 4, 8, 128), BF16), pltpu.SemaphoreType.DMA((4,))],
        far=(0,),
    )(inputs)
    z_own = lax.ppermute(z_face, "gz", swap)
    cot, z_face, inner_cot, outer_cot = call(
        prepare_cot_kernel,
        (shaped((4, 256, 1024)), shaped((128, 128)), shaped((4, 128, 128)), shaped((4, 128, 128))),
        [pltpu.VMEM((8, 32, 4, 8, 128), BF16), pltpu.SemaphoreType.DMA((8,))],
        far=(0,),
    )(cotangent.reshape(8, 32, 4, 8, 128))
    rows = lambda *parts: jnp.concatenate([part.reshape(-1, 128) for part in parts])
    outer = lax.ppermute(rows(outer, z_own, outer_cot), "gy", OUTER)
    inner = lax.ppermute(rows(inner, z_own, inner_cot), "gy", INNER)
    pay = call(
        wgrad_main_kernel,
        shaped((1024, 128), F32),
        [pltpu.VMEM((2304, 1024), BF16), pltpu.VMEM((1728, 256), F32)],
        flops=2 * 1728 * 256 * 4096,
    )(own, z_own, cot)
    pay, weight_t = lax.optimization_barrier((pay, weight_t))
    for_up, for_grad = call(
        weights_kernel, (shaped((256, 1728)), shaped((64, 2048))), [pltpu.VMEM((2048, 64), BF16)]
    )(weight_t)
    inner, outer, for_up, for_grad, pay = lax.optimization_barrier((inner, outer, for_up, for_grad, pay))
    face = shaped((4, 64, 128))
    left, right, low, high, z_all = call(
        side_in_kernel, (shaped((64, 1408)), shaped((64, 1408)), face, face, shaped((64, 128)))
    )(own, z_own, inner, outer)
    left, right = lax.ppermute(left, "gx", x_up), lax.ppermute(right, "gx", x_down)
    pay = call(
        wgrad_y_kernel,
        shaped((1024, 128), F32),
        [pltpu.VMEM((768, 128), BF16), pltpu.VMEM((2, 576, 256), F32)],
        flops=2 * 1152 * 256 * 512,
    )(low, high, z_all, cot, pay)
    face = shaped((4, 128, 128))
    pay, z_face = lax.optimization_barrier((pay, z_face))
    low_cot, high_cot, z_face = call(side_cot_kernel, (face, face, shaped((128, 128))))(z_face, inner, outer)
    z_cot = lax.ppermute(z_face, "gz", swap)
    up_shape = jax.ShapeDtypeStruct((8, 32, 4, 8, 128), BF16)
    up_scratch = [pltpu.VMEM((2, 8, 32, 8, 128), BF16), pltpu.SemaphoreType.DMA((2, 8))]
    inside = call(up_inside_kernel, up_shape, [pltpu.VMEM((2304, 1024), BF16), *up_scratch], flops=2 * 1728 * 256 * 2048)(
        own, low, high, z_all, for_up
    )
    left, right, z_cot, inside, pay = lax.optimization_barrier((left, right, z_cot, inside, pay))
    keep, give = call(
        wgrad_edge_kernel, (shaped((512, 128), F32),) * 2, [pltpu.VMEM((1152, 1024), BF16)], flops=2 * 1152 * 128 * 1024
    )(left, right, cot, pay)
    up_work = call(
        up_outside_kernel,
        up_shape,
        [pltpu.VMEM((3456, 1024), BF16), *up_scratch],
        2 * 1728 * 256 * 2048,
        (6,),
        {6: 0},
    ), (own, left, right, low, high, z_all, inside, for_up)
    grad_work = call(
        igrad_kernel,
        jax.ShapeDtypeStruct((64, 4, 8, 128), BF16),
        [pltpu.VMEM((5120, 1024), BF16), pltpu.VMEM((4, 64, 8, 128), BF16), pltpu.SemaphoreType.DMA((4,))],
        flops=2 * 2048 * 256 * 4096,
    )

    block, one, two, three = call(split_kernel, (shaped((128, 128), F32),) * 4)(keep, send(give, 0, 1, 0))
    along_x = ((0, 0, 1), (0, 8, 0), (0, 8, 1))
    (one, two, three), last = lax.optimization_barrier(((one, two, three), z_cot))
    got = [send(part, *flip) for part, flip in zip((one, two, three), along_x)]
    cot_left, cot_right = call(sides_cot_kernel, (shaped((128, 1408)), shaped((128, 1408))), flops=2 * 1728 * 256 * 2048)(
        cot, low_cot, high_cot, last
    )
    cot_left, cot_right = lax.ppermute(cot_left, "gx", x_up), lax.ppermute(cot_right, "gx", x_down)
    block = (block + got[0]) + (got[1] + got[2])
    along_y, along_z = ((1, 0, 0), (2, 0, 0), (3, 0, 0)), ((0, 2, 0), (0, 4, 0), (0, 6, 0))
    (block, *_), got, (up,) = beside([block] * 3, along_z, up_work)
    block = (block + got[0]) + (got[1] + got[2])
    grad_work = grad_work, (cot, cot_left, cot_right, low_cot, high_cot, z_cot, for_grad)
    (block, *_), got, (grad,) = beside([block] * 3, along_y, grad_work)
    block = (block + got[0]) + (got[1] + got[2])
    mine = [block] + [send(block, *flip) for flip in along_x]
    other = [send(part, 0, 1, 0) for part in mine]
    factor = 1.0 / math.sqrt(4 * 16 * 2 * inputs.shape[1] * inputs.shape[2] * inputs.shape[3])
    weight_grad = call(
        functools.partial(finish_kernel, factor=factor),
        jax.ShapeDtypeStruct((4, 4, 4, 32, 64), F32),
        [pltpu.VMEM((4, 4, 4, 32, 64), F32), pltpu.SemaphoreType.DMA((8,))],
    )(
        *mine, *other
    )
    return up.reshape(2, 2, 2, 32, 4, 8, 128), grad, weight_grad.transpose(0, 1, 2, 4, 3)


def solution(mesh):
    placed = (P(None, "gx", "gy", "gz"), P(), P(None, None, None, None, "gx", "gy", "gz"))
    return jax.shard_map(
        body,
        mesh=mesh,
        in_specs=placed,
        out_specs=(P(None, None, None, None, "gx", "gy", "gz"), P(None, "gx", "gy", "gz"), P()),
        check_vma=False,
    )
```
